768 devices in a mesh: seq: 96 (over x, z, core), head: 8 (over y).
Axes of the slice: x: 4, y: 8, z: 12, core: 2. Of those that a mesh axis runs over, the one named last changes fastest.
Arguments:
- query: bfloat16 [24576, 2048], P('seq', 'head'), may hold values from -6 to 6
- key: bfloat16 [24576, 2048], P('seq', 'head'), may hold values from -6 to 6
- value: bfloat16 [24576, 2048], P('seq', 'head'), may hold values from -6 to 6
- grad_out: bfloat16 [24576, 2048], P(('seq', 'head')), may hold values from -6 to 6
Outputs:
- grad_query: bfloat16 [24576, 2048], P('seq', 'head')
- grad_key: bfloat16 [24576, 2048], P('seq', 'head')
- grad_value: bfloat16 [24576, 2048], P('seq', 'head')
The draws below stay inside these ranges and needn't reach their ends.
All inputs are finite; a program needn't handle non-finite values.
Results may differ from the reference program's by a relative error of at most 0.0049.
Values may be sent and summed in bfloat16 or wider, within the bound.
No kernel may reach another device: no remote copies, remote signals or barrier semaphores. Data moves between devices by JAX's collectives and lax.ppermute only.
A program may use at most 64 MiB of HBM per device.

```python
import math
import jax
import jax.numpy as jnp
from jax import lax

H = 16
DH = 128
TOK_DEV = 256
TOKENS = 24576


def shard_levels(key, shape, cuts, low, top_value):
    loudness, own = 1.0, jax.random.fold_in(key, 6)
    for position, shards_of in cuts:
        draws = jnp.exp(jax.random.uniform(jax.random.fold_in(own, position), (shards_of,), jnp.float32, low / len(cuts), top_value / len(cuts)))
        loudness = loudness * jnp.repeat(draws, shape[position] // shards_of).reshape([-1 if axis == position else 1 for axis in range(len(shape))])
    return loudness


def scatter_about(own_key, dims, scale, bound, shards=(), held_as=jnp.bfloat16):
    array = scale * jax.random.normal(own_key, dims, jnp.float32)
    if shards:
        array = array * shard_levels(own_key, dims, shards, -0.22, 0.18)
    return jnp.clip(array, -bound, bound).astype(held_as)


def setup_inputs(seed: int = 0) -> dict:
    key_of = jax.random.split(jax.random.key(seed), 5)
    return {
        "query": scatter_about(key_of[0], (TOKENS, H * DH), 1.0, 6.0, ((0, 96), (1, 8))),
        "key": scatter_about(key_of[1], (TOKENS, H * DH), 1.0, 6.0, ((0, 96), (1, 8))),
        "value": scatter_about(key_of[2], (TOKENS, H * DH), 1.0, 6.0, ((0, 96), (1, 8))),
        "grad_out": scatter_about(key_of[3], (TOKENS, H * DH), 1.0, 6.0, ((0, 768),)),
    }


def one_head(parts):
    scale = 1.0 / math.sqrt(DH * TOKENS)
    qrows, krows, vrows, grows = [p.astype(jnp.float32) for p in parts]
    kv_state = jnp.einsum('ntd,nte->nde', krows, vrows)
    qg_state = jnp.einsum('ntd,nte->nde', qrows, grows)
    zero_state = jnp.zeros_like(kv_state[:1])
    before = jnp.concatenate([zero_state, jnp.cumsum(kv_state, 0)[:-1]], 0)
    after = jnp.concatenate([jnp.cumsum(qg_state[::-1], 0)[:-1][::-1], zero_state], 0)
    before = lax.optimization_barrier(before.astype(jnp.bfloat16)).astype(jnp.float32)
    after = lax.optimization_barrier(after.astype(jnp.bfloat16)).astype(jnp.float32)
    rowidx = jnp.arange(TOK_DEV, dtype=jnp.int32)
    causal = rowidx[:, None] >= rowidx[None, :]
    score_go = jnp.where(causal, jnp.einsum('ntd,nsd->nts', grows, vrows), 0.0)
    score_qk = jnp.where(causal, jnp.einsum('ntd,nsd->nts', qrows, krows), 0.0)
    score_go = lax.optimization_barrier(score_go.astype(jnp.bfloat16)).astype(jnp.float32)
    score_qk = lax.optimization_barrier(score_qk.astype(jnp.bfloat16)).astype(jnp.float32)
    dquery = jnp.einsum('nts,nsd->ntd', score_go, krows) + jnp.einsum('nte,nde->ntd', grows, before)
    dkey = jnp.einsum('nts,ntd->nsd', score_go, qrows) + jnp.einsum('nte,nde->ntd', vrows, after)
    dvalue = jnp.einsum('nts,nte->nse', score_qk, grows) + jnp.einsum('ntd,nde->nte', krows, after)
    return ((dquery * scale).astype(jnp.bfloat16), (dkey * scale).astype(jnp.bfloat16), (dvalue * scale).astype(jnp.bfloat16))

def reference(query, key, value, grad_out):
    segments = TOKENS // TOK_DEV

    def split(x):
        return x.reshape(segments, TOK_DEV, H, DH).transpose(2, 0, 1, 3)

    def join(x):
        return x.transpose(1, 2, 0, 3).reshape(TOKENS, H * DH)
    dquery, dkey, dvalue = lax.map(one_head, (split(query), split(key), split(value), split(grad_out)))
    return (join(dquery), join(dkey), join(dvalue))
```

```python
import math

import jax
import jax.numpy as jnp
from jax import lax
from jax.sharding import Mesh
from jax.sharding import PartitionSpec as P

DH = 128
X, Z, C = 4, 12, 2


def local(query, key, value, grad_out):
    x, z, c = (lax.axis_index(axis) for axis in ("x", "z", "c"))
    local_grad = lax.all_to_all(grad_out, "head", split_axis=1, concat_axis=0, tiled=True)
    tokens_here = query.shape[0]
    heads_here = query.shape[1] // DH

    def by_head(x):
        return x.reshape(tokens_here, heads_here, DH).transpose(1, 0, 2)

    query_rows = by_head(query)
    key_rows = by_head(key)
    value_rows = by_head(value)
    grad_rows = by_head(local_grad)
    scale = 1.0 / math.sqrt(DH * tokens_here * X * Z * C)
    kv_state = jnp.einsum("htd,hte->hde", key_rows, value_rows, preferred_element_type=jnp.float32)
    qg_state = jnp.einsum("htd,hte->hde", query_rows, grad_rows, preferred_element_type=jnp.float32)
    first = c == 0
    own = jnp.where(first, kv_state, qg_state)
    other = jnp.where(first, qg_state, kv_state).astype(jnp.bfloat16)

    def from_other_core(array):
        both = lax.all_gather(array, "c")
        return jnp.where(first, both[1], both[0])

    pair = own + from_other_core(other).astype(jnp.float32)
    along_z = lax.all_gather(pair.astype(jnp.bfloat16), "z").astype(jnp.float32)
    places = jnp.arange(Z)
    wanted = jnp.where(first, places < z, places > z)[:, None, None, None]
    inside = jnp.sum(jnp.where(wanted, along_z, 0.0), axis=0)
    plane = jnp.sum(along_z, axis=0).astype(jnp.bfloat16)
    along_x = lax.all_to_all(
        jnp.broadcast_to(plane[None], (X, *plane.shape)), "x", 0, 0, tiled=True
    ).astype(jnp.float32)
    places = jnp.arange(X)
    wanted = jnp.where(first, places < x, places > x)[:, None, None, None]
    mine = inside + jnp.sum(jnp.where(wanted, along_x, 0.0), axis=0)
    sent = from_other_core((mine + own).astype(jnp.bfloat16))
    mine = mine.astype(jnp.bfloat16)
    before_half = jnp.where(first, mine, sent)
    after_half = jnp.where(first, sent, mine)

    rowidx = lax.broadcasted_iota(jnp.int32, (tokens_here, tokens_here), 0)
    colidx = lax.broadcasted_iota(jnp.int32, (tokens_here, tokens_here), 1)
    causal = (rowidx >= colidx)[None, :, :]
    score_go = jnp.einsum("htd,hsd->hts", grad_rows, value_rows, preferred_element_type=jnp.float32)
    score_go = jnp.where(causal, score_go, 0.0).astype(jnp.bfloat16)
    score_qk = jnp.einsum("htd,hsd->hts", query_rows, key_rows, preferred_element_type=jnp.float32)
    score_qk = jnp.where(causal, score_qk, 0.0).astype(jnp.bfloat16)
    dquery = jnp.einsum("hts,hsd->htd", score_go, key_rows, preferred_element_type=jnp.float32)
    dquery = dquery + jnp.einsum(
        "hte,hde->htd", grad_rows, before_half, preferred_element_type=jnp.float32
    )
    dkey = jnp.einsum("hts,htd->hsd", score_go, query_rows, preferred_element_type=jnp.float32)
    dkey = dkey + jnp.einsum(
        "hte,hde->htd", value_rows, after_half, preferred_element_type=jnp.float32
    )
    dvalue = jnp.einsum("hts,hte->hse", score_qk, grad_rows, preferred_element_type=jnp.float32)
    dvalue = dvalue + jnp.einsum(
        "htd,hde->hte", key_rows, after_half, preferred_element_type=jnp.float32
    )

    def by_token(x):
        return (
            (x * scale)
            .astype(jnp.bfloat16)
            .transpose(1, 0, 2)
            .reshape(tokens_here, heads_here * DH)
        )

    return (by_token(dquery), by_token(dkey), by_token(dvalue))


def solution(mesh):
    split = Mesh(mesh.devices.reshape(X, Z, C, -1), ("x", "z", "c", "head"))
    rows = ("x", "z", "c")
    placed = (P(rows, "head"),) * 3
    return jax.shard_map(
        local,
        mesh=split,
        in_specs=(*placed, P((*rows, "head"), None)),
        out_specs=placed,
        check_vma=False,
    )
```

```python
import functools
import math

import jax
import jax.numpy as jnp
from jax import lax
from jax.experimental import pallas as pl
from jax.experimental.pallas import tpu as pltpu
from jax.sharding import Mesh
from jax.sharding import PartitionSpec as P

DH = 128
X, ZH, ZL, C = 4, 3, 4, 2
FAR = X * ZH
f32, bf16 = jnp.float32, jnp.bfloat16
VMEM = pl.BlockSpec(memory_space=pltpu.VMEM)
SMEM = pl.BlockSpec(memory_space=pltpu.SMEM)


def call(kernel, name, outs, *args, scalars=0, flops=1_000_000):
    moved = sum(a.size * a.dtype.itemsize for a in args[scalars:])
    moved += sum(math.prod(shape) * jnp.dtype(dtype).itemsize for shape, dtype in outs)
    out = pl.pallas_call(
        kernel,
        out_shape=[jax.ShapeDtypeStruct(shape, dtype) for shape, dtype in outs],
        in_specs=[SMEM] * scalars + [VMEM] * (len(args) - scalars),
        out_specs=[VMEM] * len(outs),
        cost_estimate=pl.CostEstimate(flops=flops, bytes_accessed=moved, transcendentals=0),
        name=name,
    )(*args)
    return out[0] if len(outs) == 1 else out


def dot(a, b, over_a, over_b):
    return lax.dot_general(a, b, (((over_a,), (over_b,)), ((), ())), preferred_element_type=f32)


def head(h):
    return slice(h * DH, (h + 1) * DH)


def spread_kernel(grad_ref, out_ref):
    parts, _, width = out_ref.shape
    for j in range(parts):
        out_ref[j] = grad_ref[:, j * width : (j + 1) * width]


def states_kernel(query_ref, key_ref, value_ref, grad_ref, out_ref):
    for h in range(2):
        out_ref[0, h] = dot(key_ref[:, head(h)], value_ref[:, head(h)], 0, 0)
        out_ref[1, h] = dot(query_ref[:, head(h)], grad_ref[:, head(h)], 0, 0)


def pair_kernel(place_ref, both_ref, out_ref):
    c = place_ref[0]
    for kind in range(2):
        pair = (both_ref[0, kind, c] + both_ref[1, kind, c]).astype(bf16)
        for j in range(ZL):
            out_ref[j, kind] = pair


def blocks_kernel(place_ref, near_ref, out_ref):
    far = place_ref[2]
    block = [sum(near_ref[j, kind].astype(f32) for j in range(ZL)).astype(bf16) for kind in range(2)]
    for p in range(FAR):
        later = far < p

        @pl.when(later)
        def _():
            out_ref[p] = block[0]

        @pl.when(jnp.logical_not(later))
        def _():
            out_ref[p] = block[1]


def inside_kernel(place_ref, both_ref, near_ref, out_ref):
    c, near = place_ref[0], place_ref[1]
    zero = jnp.zeros((DH, DH), f32)
    before = sum(jnp.where(j < near, near_ref[j, 0].astype(f32), zero) for j in range(ZL))
    after = sum(jnp.where(j > near, near_ref[j, 1].astype(f32), zero) for j in range(ZL))
    out_ref[0, 0] = before
    out_ref[1, 0] = before + both_ref[0, 0, c]
    out_ref[0, 1] = after + both_ref[1, 1, c]
    out_ref[1, 1] = after


def local_kernel(query_ref, key_ref, value_ref, grad_ref, dquery_ref, dkey_ref, dvalue_ref):
    tokens = query_ref.shape[0]
    rowidx = lax.broadcasted_iota(jnp.int32, (tokens, tokens), 0)
    colidx = lax.broadcasted_iota(jnp.int32, (tokens, tokens), 1)
    causal = rowidx >= colidx
    for h in range(2):
        q, k, v, g = (r[:, head(h)] for r in (query_ref, key_ref, value_ref, grad_ref))
        score_go = jnp.where(causal, dot(g, v, 1, 1), 0.0).astype(bf16)
        score_qk = jnp.where(causal, dot(q, k, 1, 1), 0.0).astype(bf16)
        dquery_ref[:, head(h)] = dot(score_go, k, 1, 0)
        dkey_ref[:, head(h)] = dot(score_go, q, 0, 0)
        dvalue_ref[:, head(h)] = dot(score_qk, g, 0, 0)


def prefix_kernel(place_ref, far_ref, inside_ref, out_ref):
    far = place_ref[2]
    zero = jnp.zeros((DH, DH), f32)
    before, after = zero, zero
    for p in range(FAR):
        block = far_ref[p].astype(f32)
        before = before + jnp.where(p < far, block, zero)
        after = after + jnp.where(p > far, block, zero)
    for c in range(2):
        out_ref[c, 0] = (inside_ref[c, 0] + before).astype(bf16)
        out_ref[c, 1] = (inside_ref[c, 1] + after).astype(bf16)


def end_kernel(scale, place_ref, key_ref, value_ref, grad_ref, states_ref, *refs):
    local_refs, out_refs = refs[:3], refs[3:]
    c = place_ref[0]
    for h in range(2):
        before, after = states_ref[h, c, 0], states_ref[h, c, 1]
        k, v, g = (r[:, head(h)] for r in (key_ref, value_ref, grad_ref))
        far = (dot(g, before, 1, 1), dot(v, after, 1, 1), dot(k, after, 1, 0))
        for total, local, out in zip(far, local_refs, out_refs):
            out[:, head(h)] = ((total + local[:, head(h)]) * scale).astype(bf16)


def local(query, key, value, grad_out):
    tokens, width = query.shape
    heads = grad_out.shape[1] // width
    x, zh, zl, c = (lax.axis_index(axis) for axis in ("x", "zh", "zl", "c"))
    place = jnp.stack([c, zl, x * ZH + zh]).astype(jnp.int32)
    scale = 1.0 / math.sqrt(DH * tokens * X * ZH * ZL * C)

    spread = call(spread_kernel, "spread", [((heads, tokens // heads, width), bf16)], grad_out)
    grad = lax.all_to_all(spread, "head", 0, 0, tiled=True).reshape(tokens, width)
    states = call(states_kernel, "states", [((2, 2, DH, DH), f32)], query, key, value, grad)
    both = lax.all_gather(states, "c")
    pair = call(pair_kernel, "pair", [((ZL, 2, DH, DH), bf16)], place, both, scalars=1)
    near = lax.all_to_all(pair, "zl", 0, 0, tiled=True)
    block = call(blocks_kernel, "blocks", [((FAR, DH, DH), bf16)], place, near, scalars=1)
    far = lax.all_to_all(block, ("x", "zh"), 0, 0, tiled=True)
    inside = call(
        inside_kernel, "inside", [((2, 2, DH, DH), f32)], place, both, near, scalars=1
    )
    partial = call(
        local_kernel, "local", [((tokens, width), f32)] * 3, query, key, value, grad, flops=200_000_000
    )
    mine = call(prefix_kernel, "prefix", [((2, 2, DH, DH), bf16)], place, far, inside, scalars=1)
    ends = lax.all_gather(mine, "c")
    outs = call(
        functools.partial(end_kernel, scale),
        "end",
        [((tokens, width), bf16)] * 3,
        place,
        key,
        value,
        grad,
        ends,
        *partial,
        scalars=1,
    )
    return tuple(outs)


def solution(mesh):
    split = Mesh(mesh.devices.reshape(X, ZH, ZL, C, -1), ("x", "zh", "zl", "c", "head"))
    rows = ("x", "zh", "zl", "c")
    placed = (P(rows, "head"),) * 3
    return jax.shard_map(
        local,
        mesh=split,
        in_specs=(*placed, P((*rows, "head"), None)),
        out_specs=placed,
        check_vma=False,
    )
```

```python
import functools
import math

import jax
import jax.numpy as jnp
from jax import lax
from jax.experimental import pallas as pl
from jax.experimental.pallas import tpu as pltpu
from jax.sharding import Mesh
from jax.sharding import PartitionSpec as P

DH = 128
X, ZH, ZL, C = 4, 3, 4, 2
NEAR, FAR = ZL * C, X * ZH
ROOM = 8 << 20
f32, bf16 = jnp.float32, jnp.bfloat16
VMEM = pl.BlockSpec(memory_space=pltpu.VMEM)
ANY = pl.BlockSpec(memory_space=pl.ANY)


def call(kernel, name, outs, *args, space=VMEM, flops=1_000_000, scratch=()):
    moved = sum(a.size * a.dtype.itemsize for a in args)
    moved += sum(math.prod(shape) * jnp.dtype(dtype).itemsize for shape, dtype in outs)
    out = pl.pallas_call(
        kernel,
        out_shape=[jax.ShapeDtypeStruct(shape, dtype) for shape, dtype in outs],
        in_specs=[space] * len(args),
        out_specs=[space] * len(outs),
        scratch_shapes=scratch,
        compiler_params=pltpu.CompilerParams(vmem_limit_bytes=ROOM),
        cost_estimate=pl.CostEstimate(flops=flops, bytes_accessed=moved, transcendentals=0),
        name=name,
    )(*args)
    return out[0] if len(outs) == 1 else out


def dot(a, b, over_a, over_b):
    return lax.dot_general(a, b, (((over_a,), (over_b,)), ((), ())), preferred_element_type=f32)


def head(h):
    return slice(h * DH, (h + 1) * DH)


def block_index():
    return lax.axis_index("x") * ZH + lax.axis_index("zh")


def spread_kernel(grad_ref, out_ref, sems):
    parts, _, width = out_ref.shape
    copies = [
        pltpu.make_async_copy(
            grad_ref.at[:, j * width : (j + 1) * width], out_ref.at[j], sems.at[j]
        )
        for j in range(parts)
    ]
    for copy in copies:
        copy.start()
    for copy in copies:
        copy.wait()


def states_kernel(query_ref, key_ref, value_ref, grad_ref, out_ref):
    per_head, rows = NEAR // 2, 2 * DH // NEAR
    for h in range(2):
        kv = dot(key_ref[:, head(h)], value_ref[:, head(h)], 0, 0)
        qg = dot(query_ref[:, head(h)], grad_ref[:, head(h)], 0, 0)
        for kind, state in enumerate((kv, qg)):
            out_ref[h * per_head : (h + 1) * per_head, kind] = state.astype(
                out_ref.dtype
            ).reshape(per_head, rows, DH)


def blocks_kernel(near_ref, out_ref):
    me = block_index()
    kv, qg = (
        sum(near_ref[i, kind].astype(f32) for i in range(NEAR)).astype(out_ref.dtype)
        for kind in range(2)
    )
    for p in range(FAR):
        out_ref[p] = jnp.where(me < p, kv, qg)


def inside_kernel(near_ref, out_ref):
    zero = jnp.zeros(near_ref.shape[2:], f32)
    before, after = zero, zero
    for i in range(NEAR):
        last = NEAR - 1 - i
        out_ref[i, 0] = before
        out_ref[last, 1] = after
        before = before + near_ref[i, 0].astype(f32)
        after = after + near_ref[last, 1].astype(f32)


def local_kernel(query_ref, key_ref, value_ref, grad_ref, dquery_ref, dkey_ref, dvalue_ref):
    tokens = query_ref.shape[0]
    rowidx = lax.broadcasted_iota(jnp.int32, (tokens, tokens), 0)
    colidx = lax.broadcasted_iota(jnp.int32, (tokens, tokens), 1)
    causal = rowidx >= colidx
    for h in range(2):
        q, k, v, g = (r[:, head(h)] for r in (query_ref, key_ref, value_ref, grad_ref))
        score_go = jnp.where(causal, dot(g, v, 1, 1), 0.0).astype(bf16)
        score_qk = jnp.where(causal, dot(q, k, 1, 1), 0.0).astype(bf16)
        dquery_ref[:, head(h)] = dot(score_go, k, 1, 0)
        dkey_ref[:, head(h)] = dot(score_go, q, 0, 0)
        dvalue_ref[:, head(h)] = dot(score_qk, g, 0, 0)


def prefix_kernel(far_ref, inside_ref, out_ref):
    me = block_index()
    zero = jnp.zeros(far_ref.shape[1:], f32)
    before, after = zero, zero
    for p in range(FAR):
        block = far_ref[p].astype(f32)
        before = before + jnp.where(p < me, block, zero)
        after = after + jnp.where(p > me, block, zero)
    for i in range(NEAR):
        out_ref[i, 0] = (inside_ref[i, 0] + before).astype(bf16)
        out_ref[i, 1] = (inside_ref[i, 1] + after).astype(bf16)


def end_kernel(scale, key_ref, value_ref, grad_ref, states_ref, *refs):
    local_refs, out_refs = refs[:3], refs[3:]
    per_head = NEAR // 2
    for h in range(2):
        before, after = (
            states_ref[h * per_head : (h + 1) * per_head, kind].reshape(DH, DH)
            for kind in range(2)
        )
        k, v, g = (r[:, head(h)] for r in (key_ref, value_ref, grad_ref))
        far = (dot(g, before, 1, 1), dot(v, after, 1, 1), dot(k, after, 1, 0))
        for total, local, out in zip(far, local_refs, out_refs):
            out[:, head(h)] = ((total + local[:, head(h)]) * scale).astype(bf16)


def local(query, key, value, grad_out):
    tokens, width = query.shape
    heads = grad_out.shape[1] // width
    rows = 2 * DH // NEAR
    scale = 1.0 / math.sqrt(DH * tokens * X * ZH * ZL * C)

    spread = call(
        spread_kernel,
        "spread",
        [((heads, tokens // heads, width), bf16)],
        grad_out,
        space=ANY,
        scratch=[pltpu.SemaphoreType.DMA((heads,))],
    )
    grad = lax.all_to_all(spread, "head", 0, 0, tiled=True).reshape(tokens, width)
    states = call(
        states_kernel, "states", [((NEAR, 2, rows, DH), bf16)], query, key, value, grad
    )
    near = lax.all_to_all(states, ("zl", "c"), 0, 0, tiled=True)
    block = call(blocks_kernel, "blocks", [((FAR, rows, DH), bf16)], near)
    far = lax.all_to_all(block, ("x", "zh"), 0, 0, tiled=True)
    inside = call(inside_kernel, "inside", [((NEAR, 2, rows, DH), f32)], near)
    partial = call(
        local_kernel, "local", [((tokens, width), f32)] * 3, query, key, value, grad, flops=200_000_000
    )
    mine = call(prefix_kernel, "prefix", [((NEAR, 2, rows, DH), bf16)], far, inside)
    ends = lax.all_to_all(mine, ("zl", "c"), 0, 0, tiled=True)
    outs = call(
        functools.partial(end_kernel, scale),
        "end",
        [((tokens, width), bf16)] * 3,
        key,
        value,
        grad,
        ends,
        *partial,
    )
    return tuple(outs)


def solution(mesh):
    split = Mesh(mesh.devices.reshape(X, ZH, ZL, C, -1), ("x", "zh", "zl", "c", "head"))
    rows = ("x", "zh", "zl", "c")
    placed = (P(rows, "head"),) * 3
    return jax.shard_map(
        local,
        mesh=split,
        in_specs=(*placed, P((*rows, "head"), None)),
        out_specs=placed,
        check_vma=False,
    )
```

```python
import functools
import math

import jax
import jax.numpy as jnp
from jax import lax
from jax.experimental import pallas as pl
from jax.experimental.pallas import tpu as pltpu
from jax.sharding import Mesh
from jax.sharding import PartitionSpec as P

DH = 128
X, ZH, ZL, C = 4, 3, 4, 2
NEAR, FAR = ZL * C, X * ZH
ROOM = 8 << 20
NEAR_ORDER = [7, 6, 5, 4, 3, 2, 1, 0]
FAR_ORDER = [8, 11, 10, 9, 7, 6, 5, 4, 3, 2, 1, 0]
HEAD_ORDER = [4, 3, 5, 2, 6, 1, 7, 0]
HEADS = len(HEAD_ORDER)
HEAD_AT = [HEAD_ORDER.index(i) for i in range(HEADS)]
NEAR_AT = [NEAR_ORDER.index(i) for i in range(NEAR)]
NEAR_GROUPS = [[(f * NEAR) + i for i in NEAR_ORDER] for f in range(FAR)]
FAR_GROUPS = [[f * NEAR + i for f in FAR_ORDER] for i in range(NEAR)]
f32, bf16 = jnp.float32, jnp.bfloat16
VMEM = pl.BlockSpec(memory_space=pltpu.VMEM)
ANY = pl.BlockSpec(memory_space=pl.ANY)


def call(kernel, name, outs, *args, space=VMEM, flops=1_000_000, scratch=()):
    moved = sum(a.size * a.dtype.itemsize for a in args)
    moved += sum(math.prod(shape) * jnp.dtype(dtype).itemsize for shape, dtype in outs)
    out = pl.pallas_call(
        kernel,
        out_shape=[jax.ShapeDtypeStruct(shape, dtype) for shape, dtype in outs],
        in_specs=[space] * len(args),
        out_specs=[space] * len(outs),
        scratch_shapes=scratch,
        compiler_params=pltpu.CompilerParams(vmem_limit_bytes=ROOM),
        cost_estimate=pl.CostEstimate(flops=flops, bytes_accessed=moved, transcendentals=0),
        name=name,
    )(*args)
    return out[0] if len(outs) == 1 else out


def dot(a, b, over_a, over_b):
    return lax.dot_general(a, b, (((over_a,), (over_b,)), ((), ())), preferred_element_type=f32)


def head(h):
    return slice(h * DH, (h + 1) * DH)


def rows_of(grad_ref):
    return jnp.concatenate([grad_ref[HEAD_AT[t]] for t in range(HEADS)], axis=0)


def block_index():
    return lax.axis_index("seq") // NEAR


def spread_kernel(grad_ref, out_ref, sems):
    parts, _, width = out_ref.shape
    copies = [
        pltpu.make_async_copy(
            grad_ref.at[:, j * width : (j + 1) * width], out_ref.at[HEAD_AT[j]], sems.at[j]
        )
        for j in range(parts)
    ]
    for copy in copies:
        copy.start()
    for copy in copies:
        copy.wait()


def states_kernel(query_ref, key_ref, value_ref, grad_ref, out_ref):
    per_head, rows = NEAR // 2, 2 * DH // NEAR
    grad = rows_of(grad_ref)
    for h in range(2):
        kv = dot(key_ref[:, head(h)], value_ref[:, head(h)], 0, 0)
        qg = dot(query_ref[:, head(h)], grad[:, head(h)], 0, 0)
        for kind, state in enumerate((kv, qg)):
            out_ref[h * per_head : (h + 1) * per_head, kind] = state.astype(
                out_ref.dtype
            ).reshape(per_head, rows, DH)


def blocks_kernel(near_ref, out_ref):
    me = block_index()
    kv, qg = (
        sum(near_ref[i, kind].astype(f32) for i in range(NEAR)).astype(out_ref.dtype)
        for kind in range(2)
    )
    for p in range(FAR):
        out_ref[p] = jnp.where(me < FAR_ORDER[p], kv, qg)


def inside_kernel(near_ref, out_ref):
    zero = jnp.zeros(near_ref.shape[2:], f32)
    before, after = zero, zero
    for i in range(NEAR):
        last = NEAR_AT[NEAR - 1 - i]
        i = NEAR_AT[i]
        out_ref[i, 0] = before
        out_ref[last, 1] = after
        before = before + near_ref[i, 0].astype(f32)
        after = after + near_ref[last, 1].astype(f32)


def local_kernel(query_ref, key_ref, value_ref, grad_ref, dquery_ref, dkey_ref, dvalue_ref):
    tokens = query_ref.shape[0]
    rowidx = lax.broadcasted_iota(jnp.int32, (tokens, tokens), 0)
    colidx = lax.broadcasted_iota(jnp.int32, (tokens, tokens), 1)
    causal = rowidx >= colidx
    grad = rows_of(grad_ref)
    for h in range(2):
        q, k, v, g = (r[:, head(h)] for r in (query_ref, key_ref, value_ref, grad))
        score_go = jnp.where(causal, dot(g, v, 1, 1), 0.0).astype(bf16)
        score_qk = jnp.where(causal, dot(q, k, 1, 1), 0.0).astype(bf16)
        dquery_ref[:, head(h)] = dot(score_go, k, 1, 0)
        dkey_ref[:, head(h)] = dot(score_go, q, 0, 0)
        dvalue_ref[:, head(h)] = dot(score_qk, g, 0, 0)


def prefix_kernel(far_ref, inside_ref, out_ref):
    me = block_index()
    zero = jnp.zeros(far_ref.shape[1:], f32)
    before, after = zero, zero
    for p in range(FAR):
        block = far_ref[p].astype(f32)
        before = before + jnp.where(FAR_ORDER[p] < me, block, zero)
        after = after + jnp.where(FAR_ORDER[p] > me, block, zero)
    for i in range(NEAR):
        out_ref[i, 0] = (inside_ref[i, 0] + before).astype(bf16)
        out_ref[i, 1] = (inside_ref[i, 1] + after).astype(bf16)


def end_kernel(scale, key_ref, value_ref, grad_ref, states_ref, *refs):
    local_refs, out_refs = refs[:3], refs[3:]
    per_head = NEAR // 2
    grad = rows_of(grad_ref)
    for h in range(2):
        before, after = (
            states_ref[h * per_head : (h + 1) * per_head, kind].reshape(DH, DH)
            for kind in range(2)
        )
        k, v, g = (r[:, head(h)] for r in (key_ref, value_ref, grad))
        far = (dot(g, before, 1, 1), dot(v, after, 1, 1), dot(k, after, 1, 0))
        for total, local, out in zip(far, local_refs, out_refs):
            out[:, head(h)] = ((total + local[:, head(h)]) * scale).astype(bf16)


def local(query, key, value, grad_out):
    tokens, width = query.shape
    heads = grad_out.shape[1] // width
    rows = 2 * DH // NEAR
    scale = 1.0 / math.sqrt(DH * tokens * X * ZH * ZL * C)

    spread = call(
        spread_kernel,
        "spread",
        [((heads, tokens // heads, width), bf16)],
        grad_out,
        space=ANY,
        scratch=[pltpu.SemaphoreType.DMA((heads,))],
    )
    grad = lax.all_to_all(
        spread, "head", 0, 0, axis_index_groups=[HEAD_ORDER], tiled=True
    )
    states = call(
        states_kernel, "states", [((NEAR, 2, rows, DH), bf16)], query, key, value, grad
    )
    near = lax.all_to_all(states, "seq", 0, 0, axis_index_groups=NEAR_GROUPS, tiled=True)
    block = call(blocks_kernel, "blocks", [((FAR, rows, DH), bf16)], near)
    far = lax.all_to_all(block, "seq", 0, 0, axis_index_groups=FAR_GROUPS, tiled=True)
    inside = call(inside_kernel, "inside", [((NEAR, 2, rows, DH), f32)], near)
    partial = call(
        local_kernel, "local", [((tokens, width), f32)] * 3, query, key, value, grad, flops=200_000_000
    )
    mine = call(prefix_kernel, "prefix", [((NEAR, 2, rows, DH), bf16)], far, inside)
    ends = lax.all_to_all(mine, "seq", 0, 0, axis_index_groups=NEAR_GROUPS, tiled=True)
    outs = call(
        functools.partial(end_kernel, scale),
        "end",
        [((tokens, width), bf16)] * 3,
        key,
        value,
        grad,
        ends,
        *partial,
    )
    return tuple(outs)


def solution(mesh):
    placed = (P("seq", "head"),) * 3
    return jax.shard_map(
        local,
        mesh=mesh,
        in_specs=(*placed, P(("seq", "head"), None)),
        out_specs=placed,
        check_vma=False,
    )
```

```python
import functools
import math

import jax
import jax.numpy as jnp
from jax import lax
from jax.experimental import pallas as pl
from jax.experimental.pallas import tpu as pltpu
from jax.sharding import Mesh
from jax.sharding import PartitionSpec as P

DH = 128
X, ZH, ZL, C = 4, 3, 4, 2
NEAR, FAR = ZL * C, X * ZH
ROOM = 8 << 20
NEAR_ORDER = [7, 6, 5, 4, 3, 2, 1, 0]
FAR_ORDER = [8, 11, 10, 9, 7, 6, 5, 4, 3, 2, 1, 0]
HEAD_ORDER = [5, 4, 6, 3, 7, 2, 1, 0]
HEADS = len(HEAD_ORDER)
HEAD_AT = [HEAD_ORDER.index(i) for i in range(HEADS)]
BACK_ORDER = [5, 7, 6, 4, 3, 2, 1, 0]
BACK_AT = [BACK_ORDER.index(i) for i in range(NEAR)]
BACK_GROUPS = [[(f * NEAR) + i for i in BACK_ORDER] for f in range(FAR)]
NEAR_AT = [NEAR_ORDER.index(i) for i in range(NEAR)]
NEAR_GROUPS = [[(f * NEAR) + i for i in NEAR_ORDER] for f in range(FAR)]
FAR_GROUPS = [[f * NEAR + i for f in FAR_ORDER] for i in range(NEAR)]
f32, bf16 = jnp.float32, jnp.bfloat16
VMEM = pl.BlockSpec(memory_space=pltpu.VMEM)
ANY = pl.BlockSpec(memory_space=pl.ANY)


def call(kernel, name, outs, *args, space=VMEM, out_space=None, flops=1_000_000, scratch=()):
    moved = sum(a.size * a.dtype.itemsize for a in args)
    moved += sum(math.prod(shape) * jnp.dtype(dtype).itemsize for shape, dtype in outs)
    out = pl.pallas_call(
        kernel,
        out_shape=[jax.ShapeDtypeStruct(shape, dtype) for shape, dtype in outs],
        in_specs=[space] * len(args),
        out_specs=[out_space or space] * len(outs),
        scratch_shapes=scratch,
        compiler_params=pltpu.CompilerParams(vmem_limit_bytes=ROOM),
        cost_estimate=pl.CostEstimate(flops=flops, bytes_accessed=moved, transcendentals=0),
        name=name,
    )(*args)
    return out[0] if len(outs) == 1 else out


def dot(a, b, over_a, over_b):
    return lax.dot_general(a, b, (((over_a,), (over_b,)), ((), ())), preferred_element_type=f32)


def head(h):
    return slice(h * DH, (h + 1) * DH)


def rows_of(grad_ref):
    return jnp.concatenate([grad_ref[HEAD_AT[t]] for t in range(HEADS)], axis=0)


def block_index():
    return lax.axis_index("seq") // NEAR


def spread_kernel(grad_ref, out_ref, sems):
    parts, _, width = out_ref.shape
    copies = [
        pltpu.make_async_copy(
            grad_ref.at[:, j * width : (j + 1) * width], out_ref.at[HEAD_AT[j]], sems.at[j]
        )
        for j in range(parts)
    ]
    for copy in copies:
        copy.start()
    for copy in copies:
        copy.wait()


def states_kernel(query_ref, key_ref, value_ref, grad_ref, out_ref):
    per_head, rows = NEAR // 2, 2 * DH // NEAR
    grad = rows_of(grad_ref)
    for h in range(2):
        kv = dot(key_ref[:, head(h)], value_ref[:, head(h)], 0, 0)
        qg = dot(query_ref[:, head(h)], grad[:, head(h)], 0, 0)
        for kind, state in enumerate((kv, qg)):
            state = state.astype(out_ref.dtype)
            for j in range(per_head):
                out_ref[NEAR_AT[h * per_head + j], kind] = state[j * rows : (j + 1) * rows]


def blocks_kernel(near_ref, out_ref):
    me = block_index()
    kv, qg = (
        sum(near_ref[i, kind].astype(f32) for i in range(NEAR)).astype(out_ref.dtype)
        for kind in range(2)
    )
    for p in range(FAR):
        out_ref[p] = jnp.where(me < FAR_ORDER[p], kv, qg)


def prefix_kernel(far_ref, near_ref, out_ref):
    me = block_index()
    zero = jnp.zeros(far_ref.shape[1:], f32)
    before, after = zero, zero
    for p in range(FAR):
        block = far_ref[p].astype(f32)
        before = before + jnp.where(FAR_ORDER[p] < me, block, zero)
        after = after + jnp.where(FAR_ORDER[p] > me, block, zero)
    for i in range(NEAR):
        last = NEAR - 1 - i
        out_ref[BACK_AT[i], 0] = before.astype(bf16)
        out_ref[BACK_AT[last], 1] = after.astype(bf16)
        before = before + near_ref[NEAR_AT[i], 0].astype(f32)
        after = after + near_ref[NEAR_AT[last], 1].astype(f32)


def end_kernel(scale, query_ref, key_ref, value_ref, grad_ref, states_ref, *refs):
    out_refs = refs
    per_head = NEAR // 2
    tokens = query_ref.shape[0]
    rowidx = lax.broadcasted_iota(jnp.int32, (tokens, tokens), 0)
    colidx = lax.broadcasted_iota(jnp.int32, (tokens, tokens), 1)
    causal, causal_to = rowidx >= colidx, rowidx <= colidx
    grad = rows_of(grad_ref)

    def finish(which, h, total):
        out_refs[which][:, head(h)] = (total * scale).astype(bf16)

    for h in range(2):
        before, after = (
            jnp.concatenate(
                [states_ref[BACK_AT[h * per_head + j], kind] for j in range(per_head)], axis=0
            )
            for kind in range(2)
        )
        q, k, v, g = (r[:, head(h)] for r in (query_ref, key_ref, value_ref, grad))
        score_qk = jnp.where(causal_to, dot(k, q, 1, 1), 0.0).astype(bf16)
        finish(2, h, dot(score_qk, g, 1, 0) + dot(k, after, 1, 0))
        score_to = jnp.where(causal_to, dot(v, g, 1, 1), 0.0).astype(bf16)
        finish(1, h, dot(score_to, q, 1, 0) + dot(v, after, 1, 1))
        score_go = jnp.where(causal, dot(g, v, 1, 1), 0.0).astype(bf16)
        finish(0, h, dot(score_go, k, 1, 0) + dot(g, before, 1, 1))


def local(query, key, value, grad_out):
    tokens, width = query.shape
    heads = grad_out.shape[1] // width
    rows = 2 * DH // NEAR
    scale = 1.0 / math.sqrt(DH * tokens * X * ZH * ZL * C)

    spread = call(
        spread_kernel,
        "spread",
        [((heads, tokens // heads, width), bf16)],
        grad_out,
        space=ANY,
        scratch=[pltpu.SemaphoreType.DMA((heads,))],
    )
    grad = lax.all_to_all(
        spread, "head", 0, 0, axis_index_groups=[HEAD_ORDER], tiled=True
    )
    states = call(
        states_kernel, "states", [((NEAR, 2, rows, DH), bf16)], query, key, value, grad
    )
    near = lax.all_to_all(states, "seq", 0, 0, axis_index_groups=NEAR_GROUPS, tiled=True)

    block = call(blocks_kernel, "blocks", [((FAR, rows, DH), bf16)], near)
    far = lax.all_to_all(block, "seq", 0, 0, axis_index_groups=FAR_GROUPS, tiled=True)
    mine = call(prefix_kernel, "prefix", [((NEAR, 2, rows, DH), bf16)], far, near)
    ends = lax.all_to_all(mine, "seq", 0, 0, axis_index_groups=BACK_GROUPS, tiled=True)
    outs = call(
        functools.partial(end_kernel, scale),
        "end",
        [((tokens, width), bf16)] * 3,
        query,
        key,
        value,
        grad,
        ends,
        flops=218_000_000,
    )
    return tuple(outs)


def solution(mesh):
    placed = (P("seq", "head"),) * 3
    return jax.shard_map(
        local,
        mesh=mesh,
        in_specs=(*placed, P(("seq", "head"), None)),
        out_specs=placed,
        check_vma=False,
    )
```

```python
import functools
import math

import jax
import jax.numpy as jnp
from jax import lax
from jax.experimental import pallas as pl
from jax.experimental.pallas import tpu as pltpu
from jax.sharding import Mesh
from jax.sharding import PartitionSpec as P

DH = 128
X, ZH, ZL, C = 4, 3, 4, 2
NEAR, FAR = ZL * C, X * ZH
ROOM = 8 << 20
NEAR_ORDER = [7, 6, 5, 4, 3, 2, 1, 0]
FAR_ORDER = [8, 11, 10, 9, 7, 6, 5, 4, 3, 2, 1, 0]
HEAD_ORDER = [5, 4, 6, 3, 7, 2, 1, 0]
HEADS = len(HEAD_ORDER)
HEAD_AT = [HEAD_ORDER.index(i) for i in range(HEADS)]
BACK_ORDER = [5, 7, 6, 4, 3, 2, 1, 0]
BACK_AT = [BACK_ORDER.index(i) for i in range(NEAR)]
BACK_GROUPS = [[(f * NEAR) + i for i in BACK_ORDER] for f in range(FAR)]
NEAR_AT = [NEAR_ORDER.index(i) for i in range(NEAR)]
NEAR_GROUPS = [[(f * NEAR) + i for i in NEAR_ORDER] for f in range(FAR)]
FAR_GROUPS = [[f * NEAR + i for f in FAR_ORDER] for i in range(NEAR)]
f32, bf16 = jnp.float32, jnp.bfloat16
VMEM = pl.BlockSpec(memory_space=pltpu.VMEM)
ANY = pl.BlockSpec(memory_space=pl.ANY)


def call(kernel, name, outs, *args, space=VMEM, out_space=None, flops=1_000_000, scratch=()):
    moved = sum(a.size * a.dtype.itemsize for a in args)
    moved += sum(math.prod(shape) * jnp.dtype(dtype).itemsize for shape, dtype in outs)
    out = pl.pallas_call(
        kernel,
        out_shape=[jax.ShapeDtypeStruct(shape, dtype) for shape, dtype in outs],
        in_specs=[space] * len(args),
        out_specs=[out_space or space] * len(outs),
        scratch_shapes=scratch,
        compiler_params=pltpu.CompilerParams(vmem_limit_bytes=ROOM),
        cost_estimate=pl.CostEstimate(flops=flops, bytes_accessed=moved, transcendentals=0),
        name=name,
    )(*args)
    return out[0] if len(outs) == 1 else out


def dot(a, b, over_a, over_b):
    return lax.dot_general(a, b, (((over_a,), (over_b,)), ((), ())), preferred_element_type=f32)


def head(h):
    return slice(h * DH, (h + 1) * DH)


def rows_of(grad_ref):
    return jnp.concatenate([grad_ref[HEAD_AT[t]] for t in range(HEADS)], axis=0)


def block_index():
    return lax.axis_index("seq") // NEAR


def spread_kernel(grad_ref, out_ref, sems):
    parts, _, width = out_ref.shape
    copies = [
        pltpu.make_async_copy(
            grad_ref.at[:, j * width : (j + 1) * width], out_ref.at[HEAD_AT[j]], sems.at[j]
        )
        for j in range(parts)
    ]
    for copy in copies:
        copy.start()
    for copy in copies:
        copy.wait()


def states_kernel(query_ref, key_ref, value_ref, grad_ref, out_ref):
    per_head, rows = NEAR // 2, 2 * DH // NEAR
    grad = rows_of(grad_ref)
    for h in range(2):
        kv = dot(key_ref[:, head(h)], value_ref[:, head(h)], 0, 0)
        qg = dot(query_ref[:, head(h)], grad[:, head(h)], 0, 0)
        for kind, state in enumerate((kv, qg)):
            state = state.astype(out_ref.dtype)
            for j in range(per_head):
                out_ref[NEAR_AT[h * per_head + j], kind] = state[j * rows : (j + 1) * rows]


def early():
    return lax.rem(block_index(), ZH) == 0


def local_products(query_ref, key_ref, value_ref, grad_ref):
    tokens = query_ref.shape[0]
    rowidx = lax.broadcasted_iota(jnp.int32, (tokens, tokens), 0)
    colidx = lax.broadcasted_iota(jnp.int32, (tokens, tokens), 1)
    causal, causal_to = rowidx >= colidx, rowidx <= colidx
    grad = rows_of(grad_ref)
    parts, scores = [], []
    for h in range(2):
        q, k, v, g = (r[:, head(h)] for r in (query_ref, key_ref, value_ref, grad))
        parts.append((q, k, g))
        scores.append((dot(g, v, 1, 1), dot(v, g, 1, 1), dot(k, q, 1, 1)))
    products = []
    for (q, k, g), (go, go_to, qk_to) in zip(parts, scores):
        go = jnp.where(causal, go, 0.0).astype(bf16)
        go_to = jnp.where(causal_to, go_to, 0.0).astype(bf16)
        qk_to = jnp.where(causal_to, qk_to, 0.0).astype(bf16)
        products.append((dot(go, k, 1, 0), dot(go_to, q, 1, 0), dot(qk_to, g, 1, 0)))
    return products


def blocks_kernel(near_ref, query_ref, key_ref, value_ref, grad_ref, out_ref, *local_refs):
    me = block_index()
    kv, qg = (
        sum(near_ref[i, kind].astype(f32) for i in range(NEAR)).astype(out_ref.dtype)
        for kind in range(2)
    )
    for p in range(FAR):
        out_ref[p] = jnp.where(me < FAR_ORDER[p], kv, qg)

    @pl.when(early())
    def _():
        products = local_products(query_ref, key_ref, value_ref, grad_ref)
        for h in range(2):
            for product, local in zip(products[h], local_refs):
                local[:, head(h)] = product


def prefix_kernel(far_ref, near_ref, out_ref):
    me = block_index()
    zero = jnp.zeros(far_ref.shape[1:], f32)
    before, after = zero, zero
    for p in range(FAR):
        block = far_ref[p].astype(f32)
        before = before + jnp.where(FAR_ORDER[p] < me, block, zero)
        after = after + jnp.where(FAR_ORDER[p] > me, block, zero)
    for i in range(NEAR):
        last = NEAR - 1 - i
        out_ref[BACK_AT[i], 0] = before.astype(bf16)
        out_ref[BACK_AT[last], 1] = after.astype(bf16)
        before = before + near_ref[NEAR_AT[i], 0].astype(f32)
        after = after + near_ref[NEAR_AT[last], 1].astype(f32)


def end_kernel(scale, query_ref, key_ref, value_ref, grad_ref, states_ref, *refs):
    local_refs, out_refs = refs[:3], refs[3:]
    per_head = NEAR // 2

    def finish(locals_of):
        grad = rows_of(grad_ref)
        for h in range(2):
            before, after = (
                jnp.concatenate(
                    [states_ref[BACK_AT[h * per_head + j], kind] for j in range(per_head)], axis=0
                )
                for kind in range(2)
            )
            k, v, g = (r[:, head(h)] for r in (key_ref, value_ref, grad))
            far = (dot(g, before, 1, 1), dot(v, after, 1, 1), dot(k, after, 1, 0))
            for total, local, out in zip(far, locals_of(h), out_refs):
                out[:, head(h)] = ((total + local) * scale).astype(bf16)

    @pl.when(early())
    def _():
        finish(lambda h: [local[:, head(h)] for local in local_refs])

    @pl.when(jnp.logical_not(early()))
    def _():
        products = local_products(query_ref, key_ref, value_ref, grad_ref)
        finish(lambda h: products[h])


def local(query, key, value, grad_out):
    tokens, width = query.shape
    heads = grad_out.shape[1] // width
    rows = 2 * DH // NEAR
    scale = 1.0 / math.sqrt(DH * tokens * X * ZH * ZL * C)

    spread = call(
        spread_kernel,
        "spread",
        [((heads, tokens // heads, width), bf16)],
        grad_out,
        space=ANY,
        scratch=[pltpu.SemaphoreType.DMA((heads,))],
    )
    grad = lax.all_to_all(
        spread, "head", 0, 0, axis_index_groups=[HEAD_ORDER], tiled=True
    )
    states = call(
        states_kernel, "states", [((NEAR, 2, rows, DH), bf16)], query, key, value, grad
    )
    near = lax.all_to_all(states, "seq", 0, 0, axis_index_groups=NEAR_GROUPS, tiled=True)

    block, *partial = call(
        blocks_kernel,
        "blocks",
        [((FAR, rows, DH), bf16)] + [((tokens, width), f32)] * 3,
        near,
        query,
        key,
        value,
        grad,
        flops=168_000_000,
    )
    far = lax.all_to_all(block, "seq", 0, 0, axis_index_groups=FAR_GROUPS, tiled=True)
    mine = call(prefix_kernel, "prefix", [((NEAR, 2, rows, DH), bf16)], far, near)
    ends = lax.all_to_all(mine, "seq", 0, 0, axis_index_groups=BACK_GROUPS, tiled=True)
    outs = call(
        functools.partial(end_kernel, scale),
        "end",
        [((tokens, width), bf16)] * 3,
        query,
        key,
        value,
        grad,
        ends,
        *partial,
        flops=218_000_000,
    )
    return tuple(outs)


def solution(mesh):
    placed = (P("seq", "head"),) * 3
    return jax.shard_map(
        local,
        mesh=mesh,
        in_specs=(*placed, P(("seq", "head"), None)),
        out_specs=placed,
        check_vma=False,
    )
```

```python
import functools
import math

import jax
import jax.numpy as jnp
from jax import lax
from jax.experimental import pallas as pl
from jax.experimental.pallas import tpu as pltpu
from jax.sharding import Mesh
from jax.sharding import PartitionSpec as P

DH = 128
X, ZH, ZL, C = 4, 3, 4, 2
NEAR, FAR = ZL * C, X * ZH
ROOM = 8 << 20
NEAR_ORDER = [7, 6, 5, 4, 3, 2, 1, 0]
FAR_ORDER = [8, 11, 10, 9, 7, 6, 5, 4, 3, 2, 1, 0]
HEAD_ORDER = [4, 7, 6, 5, 3, 2, 1, 0]
HEADS = len(HEAD_ORDER)
HEAD_AT = [HEAD_ORDER.index(i) for i in range(HEADS)]
BACK_ORDER = [5, 7, 6, 4, 3, 2, 1, 0]
BACK_AT = [BACK_ORDER.index(i) for i in range(NEAR)]
BACK_GROUPS = [[(f * NEAR) + i for i in BACK_ORDER] for f in range(FAR)]
NEAR_AT = [NEAR_ORDER.index(i) for i in range(NEAR)]
NEAR_GROUPS = [[(f * NEAR) + i for i in NEAR_ORDER] for f in range(FAR)]
FAR_GROUPS = [[f * NEAR + i for f in FAR_ORDER] for i in range(NEAR)]
f32, bf16 = jnp.float32, jnp.bfloat16
VMEM = pl.BlockSpec(memory_space=pltpu.VMEM)
ANY = pl.BlockSpec(memory_space=pl.ANY)


def call(kernel, name, outs, *args, space=VMEM, out_space=None, flops=1_000_000, scratch=()):
    moved = sum(a.size * a.dtype.itemsize for a in args)
    moved += sum(math.prod(shape) * jnp.dtype(dtype).itemsize for shape, dtype in outs)
    out = pl.pallas_call(
        kernel,
        out_shape=[jax.ShapeDtypeStruct(shape, dtype) for shape, dtype in outs],
        in_specs=[space] * len(args),
        out_specs=[out_space or space] * len(outs),
        scratch_shapes=scratch,
        compiler_params=pltpu.CompilerParams(vmem_limit_bytes=ROOM),
        cost_estimate=pl.CostEstimate(flops=flops, bytes_accessed=moved, transcendentals=0),
        name=name,
    )(*args)
    return out[0] if len(outs) == 1 else out


def dot(a, b, over_a, over_b):
    return lax.dot_general(a, b, (((over_a,), (over_b,)), ((), ())), preferred_element_type=f32)


def head(h):
    return slice(h * DH, (h + 1) * DH)


def rows_of(grad_ref):
    return jnp.concatenate([grad_ref[HEAD_AT[t]] for t in range(HEADS)], axis=0)


def block_index():
    return lax.axis_index("seq") // NEAR


def spread_kernel(grad_ref, out_ref, sems):
    parts, _, width = out_ref.shape
    copies = [
        pltpu.make_async_copy(
            grad_ref.at[:, j * width : (j + 1) * width], out_ref.at[HEAD_AT[j]], sems.at[j]
        )
        for j in range(parts)
    ]
    for copy in copies:
        copy.start()
    for copy in copies:
        copy.wait()


def states_kernel(query_ref, key_ref, value_ref, grad_ref, out_ref):
    per_head, rows = NEAR // 2, 2 * DH // NEAR
    grad = rows_of(grad_ref)
    for h in range(2):
        kv = dot(key_ref[:, head(h)], value_ref[:, head(h)], 0, 0)
        qg = dot(query_ref[:, head(h)], grad[:, head(h)], 0, 0)
        for kind, state in enumerate((kv, qg)):
            state = state.astype(out_ref.dtype)
            for j in range(per_head):
                out_ref[NEAR_AT[h * per_head + j], kind] = state[j * rows : (j + 1) * rows]


def early():
    return lax.rem(block_index(), ZH) == 0


def local_products(query_ref, key_ref, value_ref, grad_ref):
    tokens = query_ref.shape[0]
    rowidx = lax.broadcasted_iota(jnp.int32, (tokens, tokens), 0)
    colidx = lax.broadcasted_iota(jnp.int32, (tokens, tokens), 1)
    causal, causal_to = rowidx >= colidx, rowidx <= colidx
    grad = rows_of(grad_ref)
    parts, scores = [], []
    for h in range(2):
        q, k, v, g = (r[:, head(h)] for r in (query_ref, key_ref, value_ref, grad))
        parts.append((q, k, g))
        scores.append((dot(g, v, 1, 1), dot(v, g, 1, 1), dot(k, q, 1, 1)))
    products = []
    for (q, k, g), (go, go_to, qk_to) in zip(parts, scores):
        go = jnp.where(causal, go, 0.0).astype(bf16)
        go_to = jnp.where(causal_to, go_to, 0.0).astype(bf16)
        qk_to = jnp.where(causal_to, qk_to, 0.0).astype(bf16)
        products.append((dot(go, k, 1, 0), dot(go_to, q, 1, 0), dot(qk_to, g, 1, 0)))
    return products


def blocks_kernel(near_ref, query_ref, key_ref, value_ref, grad_ref, out_ref, *local_refs):
    me = block_index()
    kv, qg = (
        sum(near_ref[i, kind].astype(f32) for i in range(NEAR)).astype(out_ref.dtype)
        for kind in range(2)
    )
    for p in range(FAR):
        out_ref[p] = jnp.where(me < FAR_ORDER[p], kv, qg)

    @pl.when(early())
    def _():
        products = local_products(query_ref, key_ref, value_ref, grad_ref)
        for h in range(2):
            for product, local in zip(products[h], local_refs):
                local[:, head(h)] = product


def prefix_kernel(far_ref, near_ref, out_ref):
    me = block_index()
    zero = jnp.zeros(far_ref.shape[1:], f32)
    before, after = zero, zero
    for p in range(FAR):
        block = far_ref[p].astype(f32)
        before = before + jnp.where(FAR_ORDER[p] < me, block, zero)
        after = after + jnp.where(FAR_ORDER[p] > me, block, zero)
    for i in range(NEAR):
        last = NEAR - 1 - i
        out_ref[BACK_AT[i], 0] = before.astype(bf16)
        out_ref[BACK_AT[last], 1] = after.astype(bf16)
        before = before + near_ref[NEAR_AT[i], 0].astype(f32)
        after = after + near_ref[NEAR_AT[last], 1].astype(f32)


def end_kernel(scale, query_ref, key_ref, value_ref, grad_ref, states_ref, *refs):
    local_refs, out_refs = refs[:3], refs[3:]
    per_head = NEAR // 2

    def finish(locals_of):
        grad = rows_of(grad_ref)
        for h in range(2):
            before, after = (
                jnp.concatenate(
                    [states_ref[BACK_AT[h * per_head + j], kind] for j in range(per_head)], axis=0
                )
                for kind in range(2)
            )
            k, v, g = (r[:, head(h)] for r in (key_ref, value_ref, grad))
            far = (dot(g, before, 1, 1), dot(v, after, 1, 1), dot(k, after, 1, 0))
            for total, local, out in zip(far, locals_of(h), out_refs):
                out[:, head(h)] = ((total + local) * scale).astype(bf16)

    @pl.when(early())
    def _():
        finish(lambda h: [local[:, head(h)] for local in local_refs])

    @pl.when(jnp.logical_not(early()))
    def _():
        products = local_products(query_ref, key_ref, value_ref, grad_ref)
        finish(lambda h: products[h])


def local(query, key, value, grad_out):
    tokens, width = query.shape
    heads = grad_out.shape[1] // width
    rows = 2 * DH // NEAR
    scale = 1.0 / math.sqrt(DH * tokens * X * ZH * ZL * C)

    spread = call(
        spread_kernel,
        "spread",
        [((heads, tokens // heads, width), bf16)],
        grad_out,
        space=ANY,
        scratch=[pltpu.SemaphoreType.DMA((heads,))],
    )
    grad = lax.all_to_all(
        spread, "head", 0, 0, axis_index_groups=[HEAD_ORDER], tiled=True
    )
    states = call(
        states_kernel, "states", [((NEAR, 2, rows, DH), bf16)], query, key, value, grad
    )
    near = lax.all_to_all(states, "seq", 0, 0, axis_index_groups=NEAR_GROUPS, tiled=True)

    block, *partial = call(
        blocks_kernel,
        "blocks",
        [((FAR, rows, DH), bf16)] + [((tokens, width), f32)] * 3,
        near,
        query,
        key,
        value,
        grad,
        flops=168_000_000,
    )
    far = lax.all_to_all(block, "seq", 0, 0, axis_index_groups=FAR_GROUPS, tiled=True)
    mine = call(prefix_kernel, "prefix", [((NEAR, 2, rows, DH), bf16)], far, near)
    ends = lax.all_to_all(mine, "seq", 0, 0, axis_index_groups=BACK_GROUPS, tiled=True)
    outs = call(
        functools.partial(end_kernel, scale),
        "end",
        [((tokens, width), bf16)] * 3,
        query,
        key,
        value,
        grad,
        ends,
        *partial,
        flops=218_000_000,
    )
    return tuple(outs)


def solution(mesh):
    placed = (P("seq", "head"),) * 3
    return jax.shard_map(
        local,
        mesh=mesh,
        in_specs=(*placed, P(("seq", "head"), None)),
        out_specs=placed,
        check_vma=False,
    )
```

```python
import functools
import math

import jax
import jax.numpy as jnp
from jax import lax
from jax.experimental import pallas as pl
from jax.experimental.pallas import tpu as pltpu
from jax.sharding import Mesh
from jax.sharding import PartitionSpec as P

DH = 128
X, ZH, ZL, C = 4, 3, 4, 2
NEAR, FAR = ZL * C, X * ZH
ROOM = 8 << 20
NEAR_ORDER = [7, 6, 5, 4, 3, 2, 1, 0]
FAR_ORDER = [8, 11, 10, 9, 7, 6, 5, 4, 3, 2, 1, 0]
HEAD_ORDER = [4, 7, 6, 5, 3, 2, 1, 0]
HEADS = len(HEAD_ORDER)
HEAD_AT = [HEAD_ORDER.index(i) for i in range(HEADS)]
BACK_ORDER = [5, 7, 6, 4, 3, 2, 1, 0]
BACK_AT = [BACK_ORDER.index(i) for i in range(NEAR)]
BACK_GROUPS = [[(f * NEAR) + i for i in BACK_ORDER] for f in range(FAR)]
NEAR_AT = [NEAR_ORDER.index(i) for i in range(NEAR)]
NEAR_GROUPS = [[(f * NEAR) + i for i in NEAR_ORDER] for f in range(FAR)]
FAR_GROUPS = [[f * NEAR + i for f in FAR_ORDER] for i in range(NEAR)]
f32, bf16 = jnp.float32, jnp.bfloat16
VMEM = pl.BlockSpec(memory_space=pltpu.VMEM)
ANY = pl.BlockSpec(memory_space=pl.ANY)


def call(kernel, name, outs, *args, space=VMEM, out_space=None, flops=1_000_000, scratch=()):
    moved = sum(a.size * a.dtype.itemsize for a in args)
    moved += sum(math.prod(shape) * jnp.dtype(dtype).itemsize for shape, dtype in outs)
    out = pl.pallas_call(
        kernel,
        out_shape=[jax.ShapeDtypeStruct(shape, dtype) for shape, dtype in outs],
        in_specs=[space] * len(args),
        out_specs=[out_space or space] * len(outs),
        scratch_shapes=scratch,
        compiler_params=pltpu.CompilerParams(vmem_limit_bytes=ROOM),
        cost_estimate=pl.CostEstimate(flops=flops, bytes_accessed=moved, transcendentals=0),
        name=name,
    )(*args)
    return out[0] if len(outs) == 1 else out


def dot(a, b, over_a, over_b):
    return lax.dot_general(a, b, (((over_a,), (over_b,)), ((), ())), preferred_element_type=f32)


def head(h):
    return slice(h * DH, (h + 1) * DH)


def rows_of(grad_ref):
    return jnp.concatenate([grad_ref[HEAD_AT[t]] for t in range(HEADS)], axis=0)


def block_index():
    return lax.axis_index("seq") // NEAR


def spread_kernel(grad_ref, out_ref, sems):
    parts, _, width = out_ref.shape
    copies = [
        pltpu.make_async_copy(
            grad_ref.at[:, j * width : (j + 1) * width], out_ref.at[HEAD_AT[j]], sems.at[j]
        )
        for j in range(parts)
    ]
    for copy in copies:
        copy.start()
    for copy in copies:
        copy.wait()


def states_kernel(query_ref, key_ref, value_ref, grad_ref, out_ref):
    per_head, rows = NEAR // 2, 2 * DH // NEAR
    grad = rows_of(grad_ref)
    for h in range(2):
        kv = dot(key_ref[:, head(h)], value_ref[:, head(h)], 0, 0)
        qg = dot(query_ref[:, head(h)], grad[:, head(h)], 0, 0)
        for kind, state in enumerate((kv, qg)):
            state = state.astype(out_ref.dtype)
            for j in range(per_head):
                out_ref[NEAR_AT[h * per_head + j], kind] = state[j * rows : (j + 1) * rows]


def early():
    return lax.rem(block_index(), ZH) == 0


def local_products(query_ref, key_ref, value_ref, grad_ref):
    tokens = query_ref.shape[0]
    rowidx = lax.broadcasted_iota(jnp.int32, (tokens, tokens), 0)
    colidx = lax.broadcasted_iota(jnp.int32, (tokens, tokens), 1)
    causal, causal_to = rowidx >= colidx, rowidx <= colidx
    grad = rows_of(grad_ref)
    parts, scores = [], []
    for h in range(2):
        q, k, v, g = (r[:, head(h)] for r in (query_ref, key_ref, value_ref, grad))
        parts.append((q, k, g))
        scores.append((dot(g, v, 1, 1), dot(v, g, 1, 1), dot(k, q, 1, 1)))
    products = []
    for (q, k, g), (go, go_to, qk_to) in zip(parts, scores):
        go = jnp.where(causal, go, 0.0).astype(bf16)
        go_to = jnp.where(causal_to, go_to, 0.0).astype(bf16)
        qk_to = jnp.where(causal_to, qk_to, 0.0).astype(bf16)
        products.append((dot(go, k, 1, 0), dot(go_to, q, 1, 0), dot(qk_to, g, 1, 0)))
    return products


def blocks_kernel(near_ref, query_ref, key_ref, value_ref, grad_ref, out_ref, *local_refs):
    me = block_index()
    kv, qg = (
        sum(near_ref[i, kind].astype(f32) for i in range(NEAR)).astype(out_ref.dtype)
        for kind in range(2)
    )
    for p in range(FAR):
        out_ref[p] = jnp.where(me < FAR_ORDER[p], kv, qg)

    @pl.when(early())
    def _():
        products = local_products(query_ref, key_ref, value_ref, grad_ref)
        for h in range(2):
            for product, local in zip(products[h], local_refs):
                local[:, head(h)] = product


def prefix_kernel(far_ref, near_ref, out_ref):
    me = block_index()
    zero = jnp.zeros(far_ref.shape[1:], f32)
    before, after = zero, zero
    for p in range(FAR):
        block = far_ref[p].astype(f32)
        before = before + jnp.where(FAR_ORDER[p] < me, block, zero)
        after = after + jnp.where(FAR_ORDER[p] > me, block, zero)
    for i in range(NEAR):
        last = NEAR - 1 - i
        out_ref[BACK_AT[i], 0] = before.astype(bf16)
        out_ref[BACK_AT[last], 1] = after.astype(bf16)
        before = before + near_ref[NEAR_AT[i], 0].astype(f32)
        after = after + near_ref[NEAR_AT[last], 1].astype(f32)


def end_kernel(scale, query_ref, key_ref, value_ref, grad_ref, states_ref, *refs):
    local_refs, out_refs, (done_ref, sems) = refs[:3], refs[3:6], refs[6:]
    per_head = NEAR // 2

    def finish(locals_of):
        copies = []
        grad = rows_of(grad_ref)
        for h in range(2):
            before, after = (
                jnp.concatenate(
                    [states_ref[BACK_AT[h * per_head + j], kind] for j in range(per_head)], axis=0
                )
                for kind in range(2)
            )
            k, v, g = (r[:, head(h)] for r in (key_ref, value_ref, grad))
            far = (dot(g, before, 1, 1), dot(v, after, 1, 1), dot(k, after, 1, 0))
            for which, (total, local) in enumerate(zip(far, locals_of(h))):
                done_ref[which, h] = ((total + local) * scale).astype(bf16)
                copy = pltpu.make_async_copy(
                    done_ref.at[which, h], out_refs[which].at[:, head(h)], sems.at[which, h]
                )
                copy.start()
                copies.append(copy)
        for copy in copies:
            copy.wait()

    @pl.when(early())
    def _():
        finish(lambda h: [local[:, head(h)] for local in local_refs])

    @pl.when(jnp.logical_not(early()))
    def _():
        products = local_products(query_ref, key_ref, value_ref, grad_ref)
        finish(lambda h: products[h])


def local(query, key, value, grad_out):
    tokens, width = query.shape
    heads = grad_out.shape[1] // width
    rows = 2 * DH // NEAR
    scale = 1.0 / math.sqrt(DH * tokens * X * ZH * ZL * C)

    spread = call(
        spread_kernel,
        "spread",
        [((heads, tokens // heads, width), bf16)],
        grad_out,
        space=ANY,
        scratch=[pltpu.SemaphoreType.DMA((heads,))],
    )
    grad = lax.all_to_all(
        spread, "head", 0, 0, axis_index_groups=[HEAD_ORDER], tiled=True
    )
    states = call(
        states_kernel, "states", [((NEAR, 2, rows, DH), bf16)], query, key, value, grad
    )
    near = lax.all_to_all(states, "seq", 0, 0, axis_index_groups=NEAR_GROUPS, tiled=True)

    block, *partial = call(
        blocks_kernel,
        "blocks",
        [((FAR, rows, DH), bf16)] + [((tokens, width), f32)] * 3,
        near,
        query,
        key,
        value,
        grad,
        flops=168_000_000,
    )
    far = lax.all_to_all(block, "seq", 0, 0, axis_index_groups=FAR_GROUPS, tiled=True)
    mine = call(prefix_kernel, "prefix", [((NEAR, 2, rows, DH), bf16)], far, near)
    ends = lax.all_to_all(mine, "seq", 0, 0, axis_index_groups=BACK_GROUPS, tiled=True)
    outs = call(
        functools.partial(end_kernel, scale),
        "end",
        [((tokens, width), bf16)] * 3,
        query,
        key,
        value,
        grad,
        ends,
        *partial,
        out_space=ANY,
        flops=218_000_000,
        scratch=[pltpu.VMEM((3, 2, tokens, DH), bf16), pltpu.SemaphoreType.DMA((3, 2))],
    )
    return tuple(outs)


def solution(mesh):
    placed = (P("seq", "head"),) * 3
    return jax.shard_map(
        local,
        mesh=mesh,
        in_specs=(*placed, P(("seq", "head"), None)),
        out_specs=placed,
        check_vma=False,
    )
```
